512 devices in a mesh: rows: 32 (over z_lo, y), cols: 16 (over x, z_hi, core).
Axes of the slice: x: 4, y: 4, z: 16 (z_hi: 2, z_lo: 8; z = z_hi * 8 + z_lo), core: 2. Of those that a mesh axis runs over, the one named last changes fastest.
Arguments:
- eigenvectors: float32 [2, 16384, 6144], P(None, 'rows', 'cols'), may hold values from -6 to 6
- reflectors: float32 [32, 4, 2, 512, 256], P('rows', None, None, 'cols'), may hold values from -0.1875 to 0.1875
- tri_factors: float32 [32, 4, 2, 256, 256], P('rows', None, None, 'cols'), may hold values from -0.1875 to 0.1875
- block_order: int32 [32, 4], P('rows'), may hold values from 0 to 3, each once within a row
Outputs:
- transformed: float32 [2, 16384, 6144], P(None, 'rows', 'cols')
The draws below stay inside these ranges and needn't reach their ends.
Inputs may be any that keep to these rules, and one draw needn't show every extreme that they name: `block_order`: each row names the stored blocks 0 to 3 once each.
All inputs are finite; a program needn't handle non-finite values.
Results may differ from the reference program's by a relative error of at most 0.00011.
Values sent between devices are 32-bit elements; how exact they have to be, the bound alone decides.
A program may use at most 64 MiB of HBM per device.

```python
import jax
import jax.numpy as jnp
from jax import lax

BAND = 256
WIN = 512
TICKS = 4
ROWS = 16384
EIGS = 6144
N_ROWS = 32


def levels(own_key, dims, pieces, low, largest):
    level = 1.0
    for axis_at, shards_of in pieces:
        steps = jax.random.uniform(jax.random.fold_in(jax.random.fold_in(own_key, 6), axis_at), (shards_of,), jnp.float32, low / len(pieces), largest / len(pieces))
        level = level * jnp.repeat(jnp.exp(steps), dims[axis_at] // shards_of).reshape((-1,) + (1,) * (len(dims) - 1 - axis_at))
    return level


def centred(own_key, extent, spread, bound, split=(), dtype=jnp.bfloat16):
    factor_of = levels(own_key, extent, split, -0.22, 0.18) if split else 1.0
    values = jax.random.normal(own_key, extent, jnp.float32) * spread * factor_of
    return jnp.minimum(jnp.maximum(values, -bound), bound).astype(dtype)


def setup_inputs(seed: int = 0) -> dict:
    streams_of = jax.random.split(jax.random.key(seed), 5)
    return {
        "eigenvectors": centred(streams_of[0], (2, ROWS, EIGS), 1.0, 6.0, ((1, 32), (2, 16)), jnp.float32),
        "reflectors": centred(streams_of[1], (N_ROWS, TICKS, 2, WIN, BAND), (2 * WIN) ** -0.5, 0.1875, ((0, 32), (3, 16)), jnp.float32),
        "tri_factors": centred(streams_of[2], (N_ROWS, TICKS, 2, BAND, BAND), (4 * BAND) ** -0.5, 0.1875, ((0, 32), (3, 16)), jnp.float32),
        "block_order": jax.vmap(lambda own: jax.random.permutation(own, TICKS))(jax.random.split(streams_of[3], N_ROWS)).reshape((N_ROWS, TICKS)).astype(jnp.int32),
    }


def complex_product(left_re, left_im, right_re, right_im, form):
    first = jnp.einsum(form, left_re, right_re, precision=lax.Precision.HIGHEST)
    second = jnp.einsum(form, left_im, right_im, precision=lax.Precision.HIGHEST)
    third = jnp.einsum(form, left_re + left_im, right_re + right_im, precision=lax.Precision.HIGHEST)
    return first - second, third - first - second


def apply_block(window, vectors, factor):
    w_re, w_im = complex_product(vectors[0], -vectors[1], window[0], window[1], "sk,se->ke")
    u_re, u_im = complex_product(factor[0], factor[1], w_re, w_im, "jk,ke->je")
    d_re, d_im = complex_product(vectors[0], vectors[1], u_re, u_im, "sk,ke->se")
    return jnp.stack([window[0] - d_re, window[1] - d_im])


def reference(eigenvectors, reflectors, tri_factors, block_order):
    width = reflectors.shape[3]
    band = reflectors.shape[4]
    ticks = reflectors.shape[1]
    sections = reflectors.shape[0]
    total = eigenvectors.shape[2]
    upper = jnp.triu(jnp.ones((band, band), jnp.float32))
    batched = jax.vmap(apply_block)
    current = eigenvectors
    for tick in range(ticks):
        chosen = block_order[:, tick]
        vectors = reflectors[jnp.arange(sections), chosen]
        factors = tri_factors[jnp.arange(sections), chosen] * upper
        if tick % 2 == 0:
            blocks = current.reshape(2, sections, width, total).transpose(1, 0, 2, 3)
            blocks = batched(blocks, vectors, factors)
            current = blocks.transpose(1, 0, 2, 3).reshape(2, sections * width, total)
        else:
            middle = current[:, band:band + (sections - 1) * width]
            blocks = middle.reshape(2, sections - 1, width, total).transpose(1, 0, 2, 3)
            blocks = batched(blocks, vectors[:sections - 1], factors[:sections - 1])
            middle = blocks.transpose(1, 0, 2, 3).reshape(2, (sections - 1) * width, total)
            current = jnp.concatenate([current[:, :band], middle, current[:, band + (sections - 1) * width:]], axis=1)
    return current
```

```python
import jax
import jax.numpy as jnp
from jax import lax
from jax.experimental import pallas as pl
from jax.experimental.pallas import tpu as pltpu
from jax.sharding import PartitionSpec as P

MESH = pl.DeviceIdType.MESH
F32, BF16 = jnp.float32, jnp.bfloat16
ORDER = ((0, 0), (0, 1), (0, 2), (1, 0), (1, 1), (2, 0), (1, 2), (2, 1), (3, 0), (2, 2), (3, 1), (3, 2))


def split(a):
    hi = a.astype(BF16)
    return hi, (a - hi.astype(F32)).astype(BF16)


def make_kernel(sections, nx, ticks, win, band, lanes, chunks):
    half = win // 2
    vr = win // (4 * nx)
    fr = band // (4 * nx)

    def kernel(z_hbm, v_ref, f_ref, o_ref, out_hbm, got, zc, lifted, given, vt, vn, fn, bz, bw,
               in_sem, out_sem, zs, zr, xs, xr, ss, sr, ls, lr, rs, rr):
        r, c = lax.axis_index("rows"), lax.axis_index("cols")
        x, zh, k = c // 4, (c // 2) % 2, c % 2

        def slot(xx, zz, kk):
            return xx * 4 + zz * 2 + kk

        def at_x(d):
            return lax.rem(x + d + nx, nx)

        flip = slot(x, 1 - zh, k)
        sib = slot(x, zh, 1 - k)

        def remote(src, dst, s, rcv, dev):
            return pltpu.make_async_remote_copy(
                src_ref=src, dst_ref=dst, send_sem=s, recv_sem=rcv, device_id=dev, device_id_type=MESH)

        def zcopy(t):
            return remote(got.at[t, c], got.at[t, c], zs.at[t], zr.at[t], (r, flip))

        def xcopy(t, kind, d):
            s = slot(x, (zh, 1 - zh)[kind], k)
            return remote(got.at[t, s], got.at[t, s], xs.at[t, kind, d - 1], xr.at[t, kind, d - 1],
                          (r, slot(at_x(d), zh, k)))

        def scopy(t, kind, d):
            s = slot(at_x(-d), (zh, 1 - zh)[kind], k)
            m = kind * nx + d
            return remote(got.at[t, s], got.at[t, s], ss.at[t, m], sr.at[t, m], (r, sib))

        def heads(i, j):
            return zc.at[j, 0:half] if i == 0 else given.at[i - 1, j]

        def lift(i, j):
            return remote(heads(i, j), lifted.at[i, j], ls.at[i, j], lr.at[i, j], (r - 1, c))

        def give(i, j):
            return remote(lifted.at[i, j], given.at[i, j], rs.at[i, j], rr.at[i, j], (r + 1, c))

        barrier = pltpu.get_barrier_semaphore()
        partners = [(r, flip), (r, sib), (lax.rem(r + 1, sections), c), (lax.rem(r + sections - 1, sections), c)]
        partners += [(r, slot(at_x(d), zh, k)) for d in range(1, nx)]
        for dev in partners:
            pl.semaphore_signal(barrier, inc=1, device_id=dev, device_id_type=MESH)
        loads = []
        for j in range(chunks):
            for p in range(2):
                loads.append(pltpu.make_async_copy(
                    z_hbm.at[p, :, j * lanes:(j + 1) * lanes], zc.at[j, :, p * lanes:(p + 1) * lanes],
                    in_sem.at[2 * j + p]))
                loads[-1].start()
        for t in range(ticks):
            which = o_ref[0, t]
            got[t, c, :, 0:vr, :] = v_ref[0, which]
            got[t, c, :, vr:vr + fr, :] = f_ref[0, which]
        pl.semaphore_wait(barrier, len(partners))

        def own_out(t):
            zcopy(t).start()
            for d in range(1, nx):
                xcopy(t, 0, d).start()
            scopy(t, 0, 0).start()

        def own_in(t):
            for d in range(1, nx):
                xcopy(t, 0, d).wait_recv()
                scopy(t, 0, d).start()

        def flip_in(t):
            zcopy(t).wait_recv()
            for d in range(1, nx):
                xcopy(t, 1, d).start()
            scopy(t, 1, 0).start()

        def flip_on(t):
            for d in range(1, nx):
                xcopy(t, 1, d).wait_recv()
                scopy(t, 1, d).start()

        def all_in(t):
            for kind in range(2):
                for d in range(nx):
                    scopy(t, kind, d).wait_recv()

        def convert(t):
            for xx in range(nx):
                rows = 4 * vr
                at = xx * rows
                for p in range(2):
                    v = got[t, 4 * xx:4 * xx + 4, p, 0:vr, :].reshape(rows, band)
                    hi, lo = split(v)
                    vn[t, p * win + at:p * win + at + rows, 0:band] = hi
                    vn[t, p * win + at:p * win + at + rows, band:2 * band] = hi
                    vn[t, p * win + at:p * win + at + rows, 2 * band:3 * band] = lo
                    hi, lo = split(v.T)
                    vt[t, p * band:(p + 1) * band, at:at + rows] = hi
                    vt[t, p * band:(p + 1) * band, win + at:win + at + rows] = hi
                    vt[t, p * band:(p + 1) * band, 2 * win + at:2 * win + at + rows] = lo
            keep = lax.broadcasted_iota(jnp.int32, (band, band), 0) <= lax.broadcasted_iota(jnp.int32, (band, band), 1)
            for p in range(2):
                f = jnp.where(keep, got[t, :, p, vr:vr + fr, :].reshape(band, band), 0.0)
                hi, lo = split(f)
                fn[t, p * band:(p + 1) * band, 0:band] = hi
                fn[t, p * band:(p + 1) * band, band:2 * band] = hi
                fn[t, p * band:(p + 1) * band, 2 * band:3 * band] = lo

        def product(left, right, rows, conj):
            both = jnp.dot(left, right, preferred_element_type=F32)
            a, b = both[:rows], both[rows:]
            if conj:
                return jnp.concatenate([a[:, :lanes] + b[:, lanes:], a[:, lanes:] - b[:, :lanes]], axis=1)
            return jnp.concatenate([a[:, :lanes] - b[:, lanes:], a[:, lanes:] + b[:, :lanes]], axis=1)

        def apply(t, first, second):
            for n, ref in enumerate((first, second)):
                hi, lo = split(ref[...])
                bz[n * half:(n + 1) * half] = hi
                bz[win + n * half:win + (n + 1) * half] = lo
                bz[2 * win + n * half:2 * win + (n + 1) * half] = hi
            w = product(vt[t], bz[...], band, True)
            hi, lo = split(w)
            bw[0, 0:band], bw[0, band:2 * band], bw[0, 2 * band:3 * band] = hi, lo, hi
            u = product(fn[t], bw[0], band, False)
            hi, lo = split(u)
            bw[1, 0:band], bw[1, band:2 * band], bw[1, 2 * band:3 * band] = hi, lo, hi
            delta = product(vn[t], bw[1], win, False)
            first[...] = first[...] - delta[:half]
            second[...] = second[...] - delta[half:]

        def take(i, j):
            @pl.when(r > 0)
            def _():
                lift(i, j).wait_send()
                give(i, j).wait_recv()

            @pl.when(r == 0)
            def _():
                given[i, j] = heads(i, j)[...]

        def step(t, j):
            i = t // 2
            head, tail = heads(i, j), zc.at[j, half:win]
            if t % 2 == 0:
                if t == 0:
                    loads[2 * j].wait()
                    loads[2 * j + 1].wait()
                else:
                    take(i - 1, j)
                apply(t, head, tail)

                @pl.when(r > 0)
                def _():
                    lift(i, j).start()
            else:
                @pl.when(r < sections - 1)
                def _():
                    lift(i, j).wait_recv()
                    apply(t, tail, lifted.at[i, j])
                    give(i, j).start()

        def stores(j, part):
            rows = slice(part * half, (part + 1) * half)
            ref = zc.at[j, half:win] if part else heads(ticks // 2, j)
            return [pltpu.make_async_copy(
                ref.at[:, p * lanes:(p + 1) * lanes], out_hbm.at[p, rows, j * lanes:(j + 1) * lanes],
                out_sem.at[part, 2 * j + p]) for p in range(2)]

        def gathered(t):
            flip_on(t)
            all_in(t)
            convert(t)

        def pending(t):
            zcopy(t).wait_send()
            own_out(t + 1)

        own_out(0)
        own_in(0)
        pending(0)
        flip_in(0)
        gathered(0)
        done = set([0])
        for n, (t, j) in enumerate(ORDER):
            if t not in done:
                if t == 1:
                    own_in(1)
                    pending(1)
                    flip_in(1)
                gathered(t)
                done.add(t)
            step(t, j)
            if (t, j) == (1, 0):
                own_in(2)
                pending(2)
            if (t, j) == (1, 1):
                flip_in(2)
            if (t, j) == (2, 0):
                own_in(3)
            if (t, j) == (2, 1):
                flip_in(3)
            if t == ticks - 1:
                for copy in stores(j, 1):
                    copy.start()
        last = ticks // 2 - 1
        for j in range(chunks):
            take(last, j)
            for copy in stores(j, 0):
                copy.start()
        zcopy(ticks - 1).wait_send()
        for t in range(ticks):
            for kind in range(2):
                for d in range(nx):
                    if d:
                        xcopy(t, kind, d).wait_send()
                    scopy(t, kind, d).wait_send()

        @pl.when(r < sections - 1)
        def _():
            for i in range(ticks // 2):
                for j in range(chunks):
                    give(i, j).wait_send()
        for j in range(chunks):
            for part in range(2):
                for copy in stores(j, part):
                    copy.wait()

    return kernel


def solution(mesh):
    sections, cols = mesh.shape["rows"], mesh.shape["cols"]
    nx = cols // 4

    def shards(eigenvectors, reflectors, tri_factors, block_order):
        ticks, band = reflectors.shape[1], reflectors.shape[4]
        win = reflectors.shape[3] * cols
        lanes = 128
        chunks = eigenvectors.shape[2] // lanes
        half = win // 2
        dma = pltpu.SemaphoreType.DMA
        return pl.pallas_call(
            make_kernel(sections, nx, ticks, win, band, lanes, chunks),
            out_shape=jax.ShapeDtypeStruct(eigenvectors.shape, F32),
            in_specs=[
                pl.BlockSpec(memory_space=pl.ANY),
                pl.BlockSpec(memory_space=pltpu.VMEM),
                pl.BlockSpec(memory_space=pltpu.VMEM),
                pl.BlockSpec(memory_space=pltpu.SMEM),
            ],
            out_specs=pl.BlockSpec(memory_space=pl.ANY),
            scratch_shapes=[
                pltpu.VMEM((ticks, cols, 2, (win + band) // cols, band), F32),
                pltpu.VMEM((chunks, win, 2 * lanes), F32),
                pltpu.VMEM((ticks // 2, chunks, half, 2 * lanes), F32),
                pltpu.VMEM((ticks // 2, chunks, half, 2 * lanes), F32),
                pltpu.VMEM((ticks, 2 * band, 3 * win), BF16),
                pltpu.VMEM((ticks, 2 * win, 3 * band), BF16),
                pltpu.VMEM((ticks, 2 * band, 3 * band), BF16),
                pltpu.VMEM((3 * win, 2 * lanes), BF16),
                pltpu.VMEM((2, 3 * band, 2 * lanes), BF16),
                dma((2 * chunks,)),
                dma((2, 2 * chunks)),
                dma((ticks,)),
                dma((ticks,)),
                dma((ticks, 2, max(nx - 1, 1))),
                dma((ticks, 2, max(nx - 1, 1))),
                dma((ticks, 2 * nx)),
                dma((ticks, 2 * nx)),
                dma((ticks // 2, chunks)),
                dma((ticks // 2, chunks)),
                dma((ticks // 2, chunks)),
                dma((ticks // 2, chunks)),
            ],
            compiler_params=pltpu.CompilerParams(
                collective_id=0, has_side_effects=True, vmem_limit_bytes=60 * 2**20),
            name="sweep",
        )(eigenvectors, reflectors, tri_factors, block_order)

    return jax.shard_map(
        shards,
        mesh=mesh,
        in_specs=(
            P(None, "rows", "cols"),
            P("rows", None, None, "cols", None),
            P("rows", None, None, "cols", None),
            P("rows", None),
        ),
        out_specs=P(None, "rows", "cols"),
        check_vma=False,
    )
```

```python
import jax
import jax.numpy as jnp
from jax import lax
from jax.experimental import pallas as pl
from jax.experimental.pallas import tpu as pltpu
from jax.sharding import PartitionSpec as P

MESH = pl.DeviceIdType.MESH
F32, BF16 = jnp.float32, jnp.bfloat16
SCHEDULE = (
    "Z0", "X0", "Z1", "O0", "X1", "F0", "Z2", "O1", "G0", "X2", "A0", "S00", "F1", "Z3",
    "S01", "O2", "S02", "G1", "X3", "A1", "S10", "F2", "O3", "S11", "G2", "A2", "S20", "F3",
    "S12", "S21", "G3", "A3", "S30", "S22", "S31", "S32",
)


def split(a):
    hi = a.astype(BF16)
    return hi, (a - hi.astype(F32)).astype(BF16)


def make_kernel(sections, nx, ticks, win, band, lanes, chunks):
    half = win // 2
    vr = win // (4 * nx)
    fr = band // (4 * nx)

    def kernel(z_hbm, v_ref, f_ref, o_ref, out_hbm, got, zc, lifted, given, vt, vn, fn, bz, bw,
               in_sem, out_sem, zs, zr, xs, xr, ss, sr, ls, lr, rs, rr):
        r, c = lax.axis_index("rows"), lax.axis_index("cols")
        x, zh, k = c // 4, (c // 2) % 2, c % 2

        def slot(xx, zz, kk):
            return xx * 4 + zz * 2 + kk

        def at_x(d):
            return lax.rem(x + d + nx, nx)

        flip = slot(x, 1 - zh, k)
        sib = slot(x, zh, 1 - k)

        def remote(src, dst, s, rcv, dev):
            return pltpu.make_async_remote_copy(
                src_ref=src, dst_ref=dst, send_sem=s, recv_sem=rcv, device_id=dev, device_id_type=MESH)

        def zcopy(t):
            return remote(got.at[t, c], got.at[t, c], zs.at[t], zr.at[t], (r, flip))

        def xcopy(t, kind, d):
            s = slot(x, (zh, 1 - zh)[kind], k)
            return remote(got.at[t, s], got.at[t, s], xs.at[t, kind, d - 1], xr.at[t, kind, d - 1],
                          (r, slot(at_x(d), zh, k)))

        def scopy(t, kind, d):
            s = slot(at_x(-d), (zh, 1 - zh)[kind], k)
            m = kind * nx + d
            return remote(got.at[t, s], got.at[t, s], ss.at[t, m], sr.at[t, m], (r, sib))

        def heads(i, j):
            return zc.at[j, 0:half] if i == 0 else given.at[i - 1, j]

        def lift(i, j):
            return remote(heads(i, j), lifted.at[i, j], ls.at[i, j], lr.at[i, j], (r - 1, c))

        def give(i, j):
            return remote(lifted.at[i, j], given.at[i, j], rs.at[i, j], rr.at[i, j], (r + 1, c))

        barrier = pltpu.get_barrier_semaphore()
        partners = [(r, flip), (r, sib), (lax.rem(r + 1, sections), c), (lax.rem(r + sections - 1, sections), c)]
        partners += [(r, slot(at_x(d), zh, k)) for d in range(1, nx)]
        for dev in partners:
            pl.semaphore_signal(barrier, inc=1, device_id=dev, device_id_type=MESH)
        loads = []
        for j in range(chunks):
            for p in range(2):
                loads.append(pltpu.make_async_copy(
                    z_hbm.at[p, :, j * lanes:(j + 1) * lanes], zc.at[j, :, p * lanes:(p + 1) * lanes],
                    in_sem.at[2 * j + p]))
                loads[-1].start()
        for t in range(ticks):
            which = o_ref[0, t]
            got[t, c, :, 0:vr, :] = v_ref[0, which]
            got[t, c, :, vr:vr + fr, :] = f_ref[0, which]
        pl.semaphore_wait(barrier, len(partners))

        def own_out(t):
            for d in range(1, nx):
                xcopy(t, 0, d).start()
            scopy(t, 0, 0).start()

        def own_in(t):
            for d in range(1, nx):
                xcopy(t, 0, d).wait_recv()
                scopy(t, 0, d).start()

        def flip_in(t):
            zcopy(t).wait_recv()
            for d in range(1, nx):
                xcopy(t, 1, d).start()
            scopy(t, 1, 0).start()

        def flip_on(t):
            for d in range(1, nx):
                xcopy(t, 1, d).wait_recv()
                scopy(t, 1, d).start()

        def all_in(t):
            for kind in range(2):
                for d in range(nx):
                    scopy(t, kind, d).wait_recv()

        def convert(t):
            for xx in range(nx):
                rows = 4 * vr
                at = xx * rows
                for p in range(2):
                    v = got[t, 4 * xx:4 * xx + 4, p, 0:vr, :].reshape(rows, band)
                    hi, lo = split(v)
                    vn[t, p * win + at:p * win + at + rows, 0:band] = hi
                    vn[t, p * win + at:p * win + at + rows, band:2 * band] = hi
                    vn[t, p * win + at:p * win + at + rows, 2 * band:3 * band] = lo
                    hi, lo = split(v.T)
                    vt[t, p * band:(p + 1) * band, at:at + rows] = hi
                    vt[t, p * band:(p + 1) * band, win + at:win + at + rows] = hi
                    vt[t, p * band:(p + 1) * band, 2 * win + at:2 * win + at + rows] = lo
            keep = lax.broadcasted_iota(jnp.int32, (band, band), 0) <= lax.broadcasted_iota(jnp.int32, (band, band), 1)
            for p in range(2):
                f = jnp.where(keep, got[t, :, p, vr:vr + fr, :].reshape(band, band), 0.0)
                hi, lo = split(f)
                fn[t, p * band:(p + 1) * band, 0:band] = hi
                fn[t, p * band:(p + 1) * band, band:2 * band] = hi
                fn[t, p * band:(p + 1) * band, 2 * band:3 * band] = lo

        def product(left, rows, m, right, conj):
            a = jnp.dot(left[m * lanes:(m + 1) * lanes, :], right, preferred_element_type=F32)
            b = jnp.dot(left[rows + m * lanes:rows + (m + 1) * lanes, :], right, preferred_element_type=F32)
            if conj:
                return jnp.concatenate([a[:, :lanes] + b[:, lanes:], a[:, lanes:] - b[:, :lanes]], axis=1)
            return jnp.concatenate([a[:, :lanes] - b[:, lanes:], a[:, lanes:] + b[:, :lanes]], axis=1)

        def put(n, m, w):
            hi, lo = split(w)
            for q, part in enumerate((hi, lo, hi)):
                bw[n, q * band + m * lanes:q * band + (m + 1) * lanes] = part

        def apply(t, first, second):
            for n, ref in enumerate((first, second)):
                hi, lo = split(ref[...])
                for q, part in enumerate((hi, lo, hi)):
                    bz[q * win + n * half:q * win + (n + 1) * half] = part
            for m in range(band // lanes):
                put(0, m, product(vt.at[t], band, m, bz[...], True))
            for m in range(band // lanes):
                put(1, m, product(fn.at[t], band, m, bw[0], False))
            for m in range(win // lanes):
                ref, at = (first, m * lanes) if m * lanes < half else (second, m * lanes - half)
                ref[at:at + lanes, :] = ref[at:at + lanes, :] - product(vn.at[t], win, m, bw[1], False)

        def take(i, j):
            @pl.when(r > 0)
            def _():
                lift(i, j).wait_send()
                give(i, j).wait_recv()

            @pl.when(r == 0)
            def _():
                given[i, j] = heads(i, j)[...]

        def step(t, j):
            i = t // 2
            head, tail = heads(i, j), zc.at[j, half:win]
            if t % 2 == 0:
                if t == 0:
                    loads[2 * j].wait()
                    loads[2 * j + 1].wait()
                else:
                    take(i - 1, j)
                apply(t, head, tail)

                @pl.when(r > 0)
                def _():
                    lift(i, j).start()
            else:
                @pl.when(r < sections - 1)
                def _():
                    lift(i, j).wait_recv()
                    apply(t, tail, lifted.at[i, j])
                    give(i, j).start()

        def stores(j, part):
            rows = slice(part * half, (part + 1) * half)
            ref = zc.at[j, half:win] if part else heads(ticks // 2, j)
            return [pltpu.make_async_copy(
                ref.at[:, p * lanes:(p + 1) * lanes], out_hbm.at[p, rows, j * lanes:(j + 1) * lanes],
                out_sem.at[part, 2 * j + p]) for p in range(2)]

        def ready(t):
            all_in(t)
            convert(t)

        ops = dict(Z=lambda t: zcopy(t).start(), X=own_out, O=own_in, F=flip_in, G=flip_on, A=ready)
        for item in SCHEDULE:
            if item[0] == "S":
                t, j = int(item[1]), int(item[2])
                step(t, j)
                if t == ticks - 1:
                    for copy in stores(j, 1):
                        copy.start()
            else:
                ops[item[0]](int(item[1]))
        last = ticks // 2 - 1
        for j in range(chunks):
            take(last, j)
            for copy in stores(j, 0):
                copy.start()
        for t in range(ticks):
            zcopy(t).wait_send()
            for kind in range(2):
                for d in range(nx):
                    if d:
                        xcopy(t, kind, d).wait_send()
                    scopy(t, kind, d).wait_send()

        @pl.when(r < sections - 1)
        def _():
            for i in range(ticks // 2):
                for j in range(chunks):
                    give(i, j).wait_send()
        for j in range(chunks):
            for part in range(2):
                for copy in stores(j, part):
                    copy.wait()

    return kernel


def solution(mesh):
    sections, cols = mesh.shape["rows"], mesh.shape["cols"]
    nx = cols // 4

    def shards(eigenvectors, reflectors, tri_factors, block_order):
        ticks, band = reflectors.shape[1], reflectors.shape[4]
        win = reflectors.shape[3] * cols
        lanes = 128
        chunks = eigenvectors.shape[2] // lanes
        half = win // 2
        dma = pltpu.SemaphoreType.DMA
        return pl.pallas_call(
            make_kernel(sections, nx, ticks, win, band, lanes, chunks),
            out_shape=jax.ShapeDtypeStruct(eigenvectors.shape, F32),
            in_specs=[
                pl.BlockSpec(memory_space=pl.ANY),
                pl.BlockSpec(memory_space=pltpu.VMEM),
                pl.BlockSpec(memory_space=pltpu.VMEM),
                pl.BlockSpec(memory_space=pltpu.SMEM),
            ],
            out_specs=pl.BlockSpec(memory_space=pl.ANY),
            scratch_shapes=[
                pltpu.VMEM((ticks, cols, 2, (win + band) // cols, band), F32),
                pltpu.VMEM((chunks, win, 2 * lanes), F32),
                pltpu.VMEM((ticks // 2, chunks, half, 2 * lanes), F32),
                pltpu.VMEM((ticks // 2, chunks, half, 2 * lanes), F32),
                pltpu.VMEM((ticks, 2 * band, 3 * win), BF16),
                pltpu.VMEM((ticks, 2 * win, 3 * band), BF16),
                pltpu.VMEM((ticks, 2 * band, 3 * band), BF16),
                pltpu.VMEM((3 * win, 2 * lanes), BF16),
                pltpu.VMEM((2, 3 * band, 2 * lanes), BF16),
                dma((2 * chunks,)),
                dma((2, 2 * chunks)),
                dma((ticks,)),
                dma((ticks,)),
                dma((ticks, 2, max(nx - 1, 1))),
                dma((ticks, 2, max(nx - 1, 1))),
                dma((ticks, 2 * nx)),
                dma((ticks, 2 * nx)),
                dma((ticks // 2, chunks)),
                dma((ticks // 2, chunks)),
                dma((ticks // 2, chunks)),
                dma((ticks // 2, chunks)),
            ],
            compiler_params=pltpu.CompilerParams(
                collective_id=0, has_side_effects=True, vmem_limit_bytes=60 * 2**20),
            name="sweep",
        )(eigenvectors, reflectors, tri_factors, block_order)

    return jax.shard_map(
        shards,
        mesh=mesh,
        in_specs=(
            P(None, "rows", "cols"),
            P("rows", None, None, "cols", None),
            P("rows", None, None, "cols", None),
            P("rows", None),
        ),
        out_specs=P(None, "rows", "cols"),
        check_vma=False,
    )
```
